32 devices in a mesh: ty: 8 (over y, x, core), tx: 4 (over z).
Axes of the slice: x: 2, y: 2, z: 4, core: 2. Of those that a mesh axis runs over, the one named last changes fastest.
Arguments:
- block_input: bfloat16 [512, 192, 256], P('ty', 'tx'), may hold values from -6 to 6
- cotangent: bfloat16 [512, 192, 256], P('ty', 'tx'), may hold values from -6 to 6
- tissue: int32 [32, 12], P('ty', 'tx'), may hold values 0 or 1
- dw_weight: float32 [49, 256], replicated, may hold values from -0.875 to 0.875
- dw_bias: float32 [256], replicated, may hold values from -3 to 3
- ln_gain: float32 [256], replicated, may hold values from 0.5 to 1.5
- ln_bias: float32 [256], replicated, may hold values from -3 to 3
- w_expand: bfloat16 [256, 1024], replicated, may hold values from -0.375 to 0.375
- b_expand: float32 [1024], replicated, may hold values from -3 to 3
- w_reduce: bfloat16 [1024, 256], replicated, may hold values from -0.1875 to 0.1875
- layer_scale: float32 [256], replicated, may hold values from 0.5 to 2
Outputs:
- grad_input: bfloat16 [512, 192, 256], P('ty', 'tx')
- grad_dw: float32 [49, 256], replicated
- grad_expand: float32 [256, 1024], replicated
- grad_reduce: float32 [1024, 256], replicated
The draws below stay inside these ranges and needn't reach their ends.
Inputs may be any that keep to these rules, and one draw needn't show every extreme that they name: 1 marks a tile with tissue.
All inputs are finite; a program needn't handle non-finite values. No bound on the sum of `tissue` on one device may be relied on, other than what follows from the above.
Results may differ from the reference program's by a relative error of at most 0.007.
Values may be sent and summed in bfloat16 or wider, within the bound.
A program may use at most 256 MiB of HBM per device.

```python
import math
import jax
import jax.numpy as jnp
from jax import lax

C = 256
HID = 1024
TILE = 16
BH = 64
H = 512
W = 192
N_TY = 8


def place_ends(array, own_key, low, largest):
    spot = [jax.random.randint(jax.random.fold_in(own_key, axis), (), 0, length) for axis, length in enumerate(array.shape)]
    longest = array.shape.index(max(array.shape))
    beside = spot[:longest] + [(spot[longest] + 1) % array.shape[longest]] + spot[longest + 1:]
    return array.at[tuple(spot)].set(low).at[tuple(beside)].set(largest)


def block_levels(own_key, extent, split, low, high):
    factor_of, own = 1.0, jax.random.fold_in(own_key, 6)
    for dim, parts in split:
        heights = jnp.exp(jax.random.uniform(jax.random.fold_in(own, dim), (parts,), jnp.float32, low / len(split), high / len(split)))
        factor_of = factor_of * jnp.repeat(heights, extent[dim] // parts).reshape([-1 if axis == dim else 1 for axis in range(len(extent))])
    return factor_of


def scatter_about(own_key, extent, scale, most, split=(), held_as=jnp.bfloat16):
    values = jax.random.normal(own_key, extent, jnp.float32) * scale
    if len(split) > 0:
        values = block_levels(own_key, extent, split, -0.22, 0.18) * values
    return jnp.clip(values, min=-most, max=most).astype(held_as)


def setup_inputs(seed: int = 0) -> dict:
    streams_of = jax.random.split(jax.random.key(seed), 12)
    return {
        "block_input": scatter_about(streams_of[0], (H, W, C), 1.0, 6.0, ((0, 8), (1, 4))),
        "cotangent": scatter_about(streams_of[1], (H, W, C), 1.0, 6.0, ((0, 8), (1, 4))),
        "tissue": place_ends((jax.random.randint(streams_of[2], (H // TILE, W // TILE), 0, 2) < 1).astype(jnp.int32), jax.random.fold_in(streams_of[2], 1), 0, 1),
        "dw_weight": scatter_about(streams_of[3], (49, C), 49 ** -0.5, 0.875, (), jnp.float32),
        "dw_bias": scatter_about(streams_of[4], (C,), 0.5, 3.0, (), jnp.float32),
        "ln_gain": jnp.clip(jax.random.uniform(streams_of[5], (C,), jnp.float32, 0.5, 1.5), 0.5, 1.5),
        "ln_bias": scatter_about(streams_of[6], (C,), 0.5, 3.0, (), jnp.float32),
        "w_expand": scatter_about(streams_of[7], (C, HID), C ** -0.5, 0.375),
        "b_expand": scatter_about(streams_of[8], (HID,), 0.5, 3.0, (), jnp.float32),
        "w_reduce": scatter_about(streams_of[9], (HID, C), HID ** -0.5, 0.1875),
        "layer_scale": jnp.clip(jnp.exp(jax.random.uniform(streams_of[10], (C,), jnp.float32, math.log(0.5), math.log(2.0))), 0.5, 2.0),
    }


def depthwise(padded, kernel, rows, cols):
    total = jnp.zeros((rows, cols, padded.shape[2]), jnp.float32)
    for row_off in range(7):
        for col_off in range(7):
            window = padded[row_off:row_off + rows, col_off:col_off + cols].astype(jnp.float32)
            total = total + window * kernel[row_off * 7 + col_off]
    return total

def filter_grad(padded, grad, rows, cols):
    gradf = grad.astype(jnp.float32)
    taps = []
    for row_off in range(7):
        for col_off in range(7):
            window = padded[row_off:row_off + rows, col_off:col_off + cols].astype(jnp.float32)
            taps.append(lax.optimization_barrier(jnp.sum(window * gradf, axis=(0, 1))))
    return jnp.stack(taps)

def branch_back(pre, masked, ln_gain, ln_bias, w_expand, b_expand, w_reduce, layer_scale):
    center = pre - lax.optimization_barrier(jnp.mean(pre, axis=-1, keepdims=True))
    rstd = lax.rsqrt(lax.optimization_barrier(jnp.mean(center * center, axis=-1, keepdims=True)) + 1e-06)
    nhat = center * rstd
    normed = (nhat * ln_gain + ln_bias).astype(jnp.bfloat16)
    zvals = jnp.dot(normed, w_expand, preferred_element_type=jnp.float32) + b_expand
    cdf = 0.5 * (1.0 + jax.scipy.special.erf(zvals * 0.7071067811865476))
    hidden = (zvals * cdf).astype(jnp.bfloat16)
    go_vals = (layer_scale * masked.astype(jnp.float32)).astype(jnp.bfloat16)
    dhid = jnp.dot(go_vals, w_reduce.T, preferred_element_type=jnp.float32)
    slope = cdf + zvals * jnp.exp(-0.5 * zvals * zvals) * 0.3989422804014327
    dzvals = (dhid * slope).astype(jnp.bfloat16)
    dnorm = jnp.dot(dzvals, w_expand.T, preferred_element_type=jnp.float32) * ln_gain
    grad = rstd * (dnorm - lax.optimization_barrier(jnp.mean(dnorm, axis=-1, keepdims=True)) - nhat * lax.optimization_barrier(jnp.mean(dnorm * nhat, axis=-1, keepdims=True)))
    return (grad.astype(jnp.bfloat16), hidden, normed, go_vals, dzvals)

def reference(block_input, cotangent, tissue, dw_weight, dw_bias, ln_gain, ln_bias, w_expand, b_expand, w_reduce, layer_scale):
    mask = jnp.repeat(jnp.repeat(tissue, TILE, axis=0), TILE, axis=1)
    masked = (cotangent.astype(jnp.float32) * mask[:, :, None].astype(jnp.float32)).astype(jnp.bfloat16)
    padded = jnp.pad(block_input, ((3, 3), (3, 3), (0, 0)))
    zero = jnp.int32(0)

    def band_step(carry, index):
        acc_expand, acc_reduce, acc_dw = carry
        start = (index * BH).astype(jnp.int32)
        band = lax.dynamic_slice(padded, (start, zero, zero), (BH + 6, W + 6, C))
        pre = depthwise(band, dw_weight, BH, W) + dw_bias
        mband = lax.dynamic_slice(masked, (start, zero, zero), (BH, W, C))
        grad, hidden, normed, go_vals, dzvals = branch_back(pre.reshape(-1, C), mband.reshape(-1, C), ln_gain, ln_bias, w_expand, b_expand, w_reduce, layer_scale)
        acc_reduce = acc_reduce + jnp.dot(hidden.T, go_vals, preferred_element_type=jnp.float32)
        acc_expand = acc_expand + jnp.dot(normed.T, dzvals, preferred_element_type=jnp.float32)
        grad = grad.reshape(BH, W, C)
        acc_dw = acc_dw + filter_grad(band, grad, BH, W)
        return ((acc_expand, acc_reduce, acc_dw), grad)
    init = (jnp.zeros((C, HID), jnp.float32), jnp.zeros((HID, C), jnp.float32), jnp.zeros((49, C), jnp.float32))
    sums, grads = lax.scan(band_step, init, jnp.arange(N_TY, dtype=jnp.int32))
    grad_full = grads.reshape(H, W, C)
    grad_pad = jnp.pad(grad_full, ((3, 3), (3, 3), (0, 0)))
    flipped = dw_weight[::-1]

    def out_step(carry, index):
        start = (index * BH).astype(jnp.int32)
        band = lax.dynamic_slice(grad_pad, (start, zero, zero), (BH + 6, W + 6, C))
        cot = lax.dynamic_slice(cotangent, (start, zero, zero), (BH, W, C))
        result = cot.astype(jnp.float32) + depthwise(band, flipped, BH, W)
        return (carry, result.astype(jnp.bfloat16))
    _, outs = lax.scan(out_step, jnp.float32(0.0), jnp.arange(N_TY, dtype=jnp.int32))
    grad_input = outs.reshape(H, W, C)
    factor = 1.0 / math.sqrt(H * W)
    return (grad_input, sums[2] * factor, sums[0] * factor, sums[1] * factor)
```

```python
import functools
import math

import jax
import jax.numpy as jnp
from jax import lax
from jax.experimental import pallas as pl
from jax.experimental.pallas import tpu as pltpu
from jax.sharding import PartitionSpec as P

TILE = 16
MESH = pl.DeviceIdType.MESH
F32, BF16 = jnp.float32, jnp.bfloat16
STEPS = ((-1, 0), (1, 0), (0, -1), (0, 1), (-1, -1), (-1, 1), (1, -1), (1, 1))
PITCH = 64


def halo_bufs(cols, rows, chans):
    return [
        pltpu.VMEM((3, cols, chans), BF16),
        pltpu.VMEM((3, cols, chans), BF16),
        pltpu.VMEM((3, rows, chans), BF16),
        pltpu.VMEM((3, rows, chans), BF16),
        pltpu.VMEM((4, 3, 16, chans), BF16),
        pltpu.SemaphoreType.DMA((8,)),
        pltpu.SemaphoreType.DMA((8,)),
    ]


class Halo:
    def __init__(self, nty, ntx, block, left, right, bufs):
        self.nty, self.ntx = nty, ntx
        self.ty, self.tx = lax.axis_index("ty"), lax.axis_index("tx")
        self.block, self.left, self.right = block, left, right
        self.bufs = bufs

    def there(self, dy, dx):
        ok = None
        for step, at, count in ((dy, self.ty, self.nty), (dx, self.tx, self.ntx)):
            if step:
                one = (at > 0) if step < 0 else (at < count - 1)
                ok = one if ok is None else jnp.logical_and(ok, one)
        return ok

    def greet(self, barrier):
        count = jnp.int32(0)
        for dy, dx in STEPS:
            ok = self.there(dy, dx)

            @pl.when(ok)
            def _(dy=dy, dx=dx):
                pl.semaphore_signal(
                    barrier, inc=1, device_id=(self.ty + dy, self.tx + dx), device_id_type=MESH
                )

            count = count + jnp.where(ok, 1, 0)
        return count

    def copy(self, index):
        dy, dx = STEPS[index]
        top, bottom, left, right, corner, send, recv = self.bufs
        rows = self.block.shape[0]
        src, dst = (
            (self.block.at[0:3], bottom),
            (self.block.at[rows - 3 : rows], top),
            (self.left, right),
            (self.right, left),
            (self.left.at[:, 0:16], corner.at[3]),
            (self.right.at[:, 0:16], corner.at[2]),
            (self.left.at[:, rows - 16 : rows], corner.at[1]),
            (self.right.at[:, rows - 16 : rows], corner.at[0]),
        )[index]
        return pltpu.make_async_remote_copy(
            src_ref=src,
            dst_ref=dst,
            send_sem=send.at[index],
            recv_sem=recv.at[index],
            device_id=(self.ty + dy, self.tx + dx),
            device_id_type=MESH,
        )

    def start(self):
        for index, step in enumerate(STEPS):

            @pl.when(self.there(*step))
            def _(index=index):
                self.copy(index).start()

    def fill(self, work):
        rows, cols, chans = self.block.shape
        halves = chans // 128

        def zero(i, _):
            at = pl.multiple_of(i * PITCH, PITCH)
            work[pl.ds(at, PITCH), :] = jnp.zeros((PITCH, 128), F32)
            return 0

        for h in range(halves):
            lax.fori_loop(h * (rows + 6), h * (rows + 6) + 3, zero, 0)
            lax.fori_loop((h + 1) * (rows + 6) - 3, (h + 1) * (rows + 6), zero, 0)

        def row(i, _):
            for h in range(halves):
                at = pl.multiple_of((h * (rows + 6) + 3 + i) * PITCH, PITCH)
                work[pl.ds(at, 8), :] = jnp.zeros((8, 128), F32)
                work[pl.ds(at + 8, cols), :] = self.block[i, :, h * 128 : h * 128 + 128].astype(F32)
                work[pl.ds(at + 8 + cols, 8), :] = jnp.zeros((8, 128), F32)
            return 0

        lax.fori_loop(0, rows, row, 0)

    def finish(self, work):
        rows, cols, chans = self.block.shape
        halves = chans // 128
        top, bottom, left, right, corner, _, _ = self.bufs
        for index, (dy, dx) in enumerate(STEPS):

            @pl.when(self.there(-dy, -dx))
            def _(index=index):
                self.copy(index).wait_recv()

                for h in range(halves):
                    lanes = slice(h * 128, h * 128 + 128)
                    base = h * (rows + 6)
                    if index < 2:
                        first = 3 + rows if index == 0 else 0
                        src = bottom if index == 0 else top
                        for r in range(3):
                            work[pl.ds((base + first + r) * PITCH + 8, cols), :] = src[r, :, lanes].astype(F32)
                    elif index < 4:
                        first = 8 + cols if index == 2 else 5
                        src = right if index == 2 else left
                        for k in range(3):
                            for g in range(rows // 16):
                                vals = src[k, g * 16 : g * 16 + 16, lanes].astype(F32)
                                for s in range(2):
                                    at = (base + 3 + g * 16 + s * 8) * PITCH + first + k
                                    work[pl.ds(at, 8, stride=PITCH), :] = vals[s * 8 : s * 8 + 8]
                    else:
                        slot = 7 - index
                        low, near = slot < 2, slot % 2 == 0
                        for k in range(3):
                            vals = corner[slot, k, :, lanes].astype(F32)
                            for r in range(3):
                                row = base + (r if low else 3 + rows + r)
                                at = row * PITCH + (5 if near else 8 + cols) + k
                                pick = (13 + r) if low else r
                                work[pl.ds(at, 1), :] = vals[pick : pick + 1]

        for index, step in enumerate(STEPS):

            @pl.when(self.there(*step))
            def _(index=index):
                self.copy(index).wait_send()


def spot(t, rows, cols):
    per = (rows // 4) * (cols // 16)
    h = t // per
    rest = t % per
    r = (rest // (cols // 16)) * 4
    c = (rest % (cols // 16)) * 16
    at = pl.multiple_of((h * (rows + 6) + r) * PITCH + c, 16)
    return h, r, pl.multiple_of(c, 16), at


def conv_block(work, taps, h, at, flip):
    total = [None] * 4
    for b in range(7):
        lines = [work[pl.ds(at + r * PITCH + 5 + b, 16), :] for r in range(10)]
        for a in range(7):
            tap = a * 7 + b
            tap = 48 - tap if flip else tap
            weight = taps[pl.ds(h * 49 + tap, 1), :]
            for o in range(4):
                term = lines[o + a] * weight
                total[o] = term if total[o] is None else total[o] + term
    return total


def pre_kernel(nty, ntx, block, left, right, taps, bias, out, work, *bufs):
    rows, cols, chans = block.shape
    halo = Halo(nty, ntx, block, left, right, bufs)
    barrier = pltpu.get_barrier_semaphore()
    count = halo.greet(barrier)
    pl.semaphore_wait(barrier, count)
    halo.start()
    halo.fill(work)
    halo.finish(work)
    per = (rows // 4) * (cols // 16)
    for half in range(chans // 128):

        def step(t, _, half=half):
            _, r, c, at = spot(t, rows, cols)
            total = conv_block(work, taps, half, at, False)
            for o in range(4):
                out[r + o, pl.ds(c, 16), half * 128 : half * 128 + 128] = total[o] + bias[pl.ds(half, 1), :]
            return 0

        lax.fori_loop(half * per, (half + 1) * per, step, 0)


def post_kernel(
    nty, ntx, size, block, left, right, xblock_pad, cot, taps, sums_in,
    out, sums, dsum, work, dacc, ssend, srecv, gathered, dsend, drecv,
    s_send, s_recv, d_send, d_recv, *bufs,
):
    rows, cols, chans = block.shape
    halves = chans // 128
    halo = Halo(nty, ntx, block, left, right, bufs)
    ty, tx = halo.ty, halo.tx
    bits = [("ty", 1 << k) for k in range(nty.bit_length() - 1)]
    bits += [("tx", 1 << k) for k in range(ntx.bit_length() - 1)]
    nb = len(bits)

    def mine(k):
        axis, bit = bits[k]
        return ((ty if axis == "ty" else tx) // bit) % 2

    def partner(k):
        axis, bit = bits[k]
        step = bit - 2 * bit * mine(k)
        return (ty + step, tx) if axis == "ty" else (ty, tx + step)

    barrier = pltpu.get_barrier_semaphore()
    count = halo.greet(barrier)
    for k in range(nb):
        pl.semaphore_signal(barrier, inc=1, device_id=partner(k), device_id_type=MESH)
    pl.semaphore_wait(barrier, count + nb)
    halo.start()

    lows = [jnp.int32(0)]
    for k in range(nb):
        lows.append(lows[k] + mine(k) * (size >> (k + 1)))

    def by_chunk(length, fn):
        step = min(length, 128)

        def go(i, _):
            fn(pl.multiple_of(i * step, 16), step)
            return 0

        lax.fori_loop(0, length // step, go, 0)

    def rs_copy(k):
        length = size >> (k + 1)
        away = pl.multiple_of(lows[k] + (1 - mine(k)) * length, 16)
        return pltpu.make_async_remote_copy(
            src_ref=ssend.at[pl.ds(away, length)],
            dst_ref=srecv.at[pl.ds(size - 2 * length, length)],
            send_sem=s_send.at[k],
            recv_sem=s_recv.at[k],
            device_id=partner(k),
            device_id_type=MESH,
        )

    def rs_start(k):
        length = size >> (k + 1)
        away = lows[k] + (1 - mine(k)) * length
        source = sums_in if k == 0 else sums

        def cast(i, step):
            at = pl.multiple_of(away + i, 16)
            ssend[pl.ds(at, step), :] = source[pl.ds(at, step), :].astype(BF16)

        by_chunk(length, cast)
        rs_copy(k).start()

    def rs_end(k):
        length = size >> (k + 1)
        source = sums_in if k == 0 else sums
        rs_copy(k).wait()

        def add(i, step):
            at = pl.multiple_of(lows[k + 1] + i, 16)
            got = srecv[pl.ds(pl.multiple_of(size - 2 * length + i, 16), step), :]
            sums[pl.ds(at, step), :] = source[pl.ds(at, step), :] + got.astype(F32)

        by_chunk(length, add)

    def ag_copy(k):
        length = size >> (k + 1)
        at = pl.multiple_of(lows[k + 1], 16)
        return pltpu.make_async_remote_copy(
            src_ref=gathered.at[pl.ds(at, length)],
            dst_ref=gathered.at[pl.ds(at, length)],
            send_sem=s_send.at[nb + k],
            recv_sem=s_recv.at[nb + k],
            device_id=partner(k),
            device_id_type=MESH,
        )

    def ag_start(k):
        if k == nb - 1:
            length = size >> nb

            def cast(i, step):
                at = pl.multiple_of(lows[nb] + i, 16)
                gathered[pl.ds(at, step), :] = sums[pl.ds(at, step), :].astype(BF16)

            by_chunk(length, cast)
        ag_copy(k).start()

    def d_copy(k):
        return pltpu.make_async_remote_copy(
            src_ref=dsend.at[k],
            dst_ref=drecv.at[k],
            send_sem=d_send.at[k],
            recv_sem=d_recv.at[k],
            device_id=partner(k),
            device_id_type=MESH,
        )

    events = []
    for k in range(nb):
        events.append((functools.partial(rs_start, k), functools.partial(rs_end, k)))
    for k in reversed(range(nb)):
        events.append((functools.partial(ag_start, k), ag_copy(k).wait))
    d_events = [(d_copy(k).start, functools.partial(lambda k: d_end(k), k)) for k in range(nb)]

    def d_end(k):
        d_copy(k).wait()
        new = dsend[k] + drecv[k]
        if k + 1 < nb:
            dsend[k + 1] = new
        else:
            dsum[...] = new

    events[0][0]()
    at_event = [0, 0]

    def advance(upto, which, line):
        while at_event[which] < upto:
            e = at_event[which]
            line[e][1]()
            if e + 1 < len(line):
                line[e + 1][0]()
            at_event[which] += 1

    halo.fill(work)

    dacc[...] = jnp.zeros_like(dacc)
    blocks = halves * (rows // 4) * (cols // 16)

    def grad_step(t, _):
        h, r, c, at = spot(t, rows, cols)
        mid = pl.multiple_of(at + 3 * PITCH + 8, 8)
        gs = [work[pl.ds(mid + o * PITCH, 16), :] for o in range(4)]
        for b in range(7):
            lines = [xblock_pad[pl.ds(at + q * PITCH + 5 + b, 16), :] for q in range(10)]
            for a in range(7):
                term = lines[a] * gs[0]
                for o in range(1, 4):
                    term = term + lines[o + a] * gs[o]
                slot = pl.multiple_of((h * 49 + a * 7 + b) * 8, 8)
                dacc[pl.ds(slot, 8), :] = dacc[pl.ds(slot, 8), :] + (term[:8] + term[8:])
        return 0

    def out_step(half, t, _):
        _, r, c, at = spot(t, rows, cols)
        total = conv_block(work, taps, half, at, True)
        for o in range(4):
            lanes = slice(half * 128, half * 128 + 128)
            res = total[o] + cot[r + o, pl.ds(c, 16), lanes].astype(F32)
            out[r + o, pl.ds(c, 16), lanes] = res.astype(BF16)
        return 0

    pieces = 4
    each = blocks // pieces
    for p in range(pieces):
        lax.fori_loop(p * each, (p + 1) * each, grad_step, 0)
        advance(len(events) * (p + 1) // (2 * pieces), 0, events)

    def fold(i, _):
        at = pl.multiple_of(i * 8, 8)
        dsend[0, pl.ds(i, 1), :] = jnp.sum(dacc[pl.ds(at, 8), :], axis=0, keepdims=True)
        return 0

    dsend[0, 96:104, :] = jnp.zeros((8, 128), F32)
    lax.fori_loop(0, halves * 49, fold, 0)
    d_events[0][0]()
    halo.finish(work)
    for p in range(pieces):
        lax.fori_loop(
            p * each, (p + 1) * each, functools.partial(out_step, p * halves // pieces), 0
        )
        advance(len(events) * (pieces + p + 1) // (2 * pieces), 0, events)
        advance(nb * (p + 1) // pieces, 1, d_events)

    def widen(i, step):
        sums[pl.ds(i, step), :] = gathered[pl.ds(i, step), :].astype(F32)

    by_chunk(size, widen)


def strips(block):
    cols = block.shape[1]
    return (
        jnp.transpose(block[:, :3], (1, 0, 2)),
        jnp.transpose(block[:, cols - 3 :], (1, 0, 2)),
    )


def branch_back(pre, masked, ln_gain, ln_bias, w_expand, b_expand, w_reduce, layer_scale):
    center = pre - jnp.mean(pre, axis=-1, keepdims=True)
    rstd = lax.rsqrt(jnp.mean(center * center, axis=-1, keepdims=True) + 1e-06)
    nhat = center * rstd
    normed = (nhat * ln_gain + ln_bias).astype(BF16)
    zvals = jnp.dot(normed, w_expand, preferred_element_type=F32) + b_expand
    cdf = 0.5 * (1.0 + jax.scipy.special.erf(zvals * 0.7071067811865476))
    hidden = (zvals * cdf).astype(BF16)
    go_vals = (layer_scale * masked.astype(F32)).astype(BF16)
    dhid = jnp.dot(go_vals, w_reduce.T, preferred_element_type=F32)
    slope = cdf + zvals * jnp.exp(-0.5 * zvals * zvals) * 0.3989422804014327
    dzvals = (dhid * slope).astype(BF16)
    dnorm = jnp.dot(dzvals, w_expand.T, preferred_element_type=F32) * ln_gain
    grad = rstd * (
        dnorm
        - jnp.mean(dnorm, axis=-1, keepdims=True)
        - nhat * jnp.mean(dnorm * nhat, axis=-1, keepdims=True)
    )
    return (grad.astype(BF16), hidden, normed, go_vals, dzvals)


def body(
    nty,
    ntx,
    block_input,
    cotangent,
    tissue,
    dw_weight,
    dw_bias,
    ln_gain,
    ln_bias,
    w_expand,
    b_expand,
    w_reduce,
    layer_scale,
):
    rows, cols, chans = block_input.shape
    hid = w_expand.shape[1]
    halves = chans // 128
    padded = halves * (rows + 6) * PITCH
    taps = jnp.transpose(dw_weight.reshape(49, halves, 128), (1, 0, 2)).reshape(halves * 49, 128)
    vmem = pl.BlockSpec(memory_space=pltpu.VMEM)
    flops = 49 * 2 * rows * cols * chans
    pre, xpad = pl.pallas_call(
        functools.partial(pre_kernel, nty, ntx),
        out_shape=(
            jax.ShapeDtypeStruct((rows, cols, chans), F32),
            jax.ShapeDtypeStruct((padded, 128), F32),
        ),
        in_specs=[vmem] * 5,
        out_specs=(vmem, vmem),
        scratch_shapes=halo_bufs(cols, rows, chans),
        compiler_params=pltpu.CompilerParams(
            collective_id=0, has_side_effects=True, vmem_limit_bytes=40 << 20
        ),
        cost_estimate=pl.CostEstimate(flops=flops, bytes_accessed=16 << 20, transcendentals=0),
        name="pre",
    )(block_input, *strips(block_input), taps, dw_bias.reshape(halves, 128))

    mask = jnp.repeat(jnp.repeat(tissue, TILE, axis=0), TILE, axis=1)
    masked = (cotangent.astype(F32) * mask[:, :, None].astype(F32)).astype(BF16)
    params = (ln_gain, ln_bias, w_expand, b_expand, w_reduce, layer_scale)
    grad, hidden, normed, go_vals, dzvals = branch_back(
        pre.reshape(-1, chans), masked.reshape(-1, chans), *params
    )
    grad_core = grad.reshape(rows, cols, chans)
    local_reduce = jnp.dot(hidden.T, go_vals, preferred_element_type=F32)
    local_expand = jnp.dot(normed.T, dzvals, preferred_element_type=F32)

    wide = hid // 128
    sums_in = jnp.concatenate(
        [local_expand[:, k * 128 : (k + 1) * 128] for k in range(wide)]
        + [local_reduce[:, k * 128 : (k + 1) * 128] for k in range(halves)]
    )
    used = sums_in.shape[0]
    unit = nty * ntx * 16
    size = -(-used // unit) * unit
    if size != used:
        sums_in = jnp.pad(sums_in, ((0, size - used), (0, 0)))
    nb = (nty * ntx).bit_length() - 1
    out, sums, dsum = pl.pallas_call(
        functools.partial(post_kernel, nty, ntx, size),
        out_shape=(
            jax.ShapeDtypeStruct((rows, cols, chans), BF16),
            jax.ShapeDtypeStruct((size, 128), F32),
            jax.ShapeDtypeStruct((104, 128), F32),
        ),
        in_specs=[vmem] * 7,
        out_specs=(vmem,) * 3,
        scratch_shapes=[
            pltpu.VMEM((padded, 128), F32),
            pltpu.VMEM((halves * 49 * 8, 128), F32),
            pltpu.VMEM((size, 128), BF16),
            pltpu.VMEM((size, 128), BF16),
            pltpu.VMEM((size, 128), BF16),
            pltpu.VMEM((nb, 104, 128), F32),
            pltpu.VMEM((nb, 104, 128), F32),
            pltpu.SemaphoreType.DMA((2 * nb,)),
            pltpu.SemaphoreType.DMA((2 * nb,)),
            pltpu.SemaphoreType.DMA((nb,)),
            pltpu.SemaphoreType.DMA((nb,)),
        ]
        + halo_bufs(cols, rows, chans),
        compiler_params=pltpu.CompilerParams(
            collective_id=1, has_side_effects=True, vmem_limit_bytes=50 << 20
        ),
        cost_estimate=pl.CostEstimate(flops=2 * flops, bytes_accessed=24 << 20, transcendentals=0),
        name="post",
    )(grad_core, *strips(grad_core), xpad, cotangent, taps, sums_in)

    factor = 1.0 / math.sqrt(rows * nty * cols * ntx)
    total_expand = jnp.concatenate([sums[k * chans : (k + 1) * chans] for k in range(wide)], axis=1)
    base = wide * chans
    total_reduce = jnp.concatenate(
        [sums[base + k * hid : base + (k + 1) * hid] for k in range(halves)], axis=1
    )
    total_dw = jnp.concatenate([dsum[k * 49 : (k + 1) * 49] for k in range(halves)], axis=1)
    return (out, total_dw * factor, total_expand * factor, total_reduce * factor)


def solution(mesh):
    placed = (P("ty", "tx", None), P("ty", "tx", None), P("ty", "tx")) + (P(),) * 8
    return jax.shard_map(
        functools.partial(body, mesh.shape["ty"], mesh.shape["tx"]),
        mesh=mesh,
        in_specs=placed,
        out_specs=(P("ty", "tx", None), P(), P(), P()),
        check_vma=False,
    )
```

```python
import functools
import math

import jax
import jax.numpy as jnp
from jax import lax
from jax.experimental import pallas as pl
from jax.experimental.pallas import tpu as pltpu
from jax.sharding import PartitionSpec as P

TILE = 16
MESH = pl.DeviceIdType.MESH
F32, BF16 = jnp.float32, jnp.bfloat16
STEPS = ((-1, 0), (1, 0), (0, -1), (0, 1), (-1, -1), (-1, 1), (1, -1), (1, 1))
PITCH = 64


def halo_bufs(cols, rows, chans):
    return [
        pltpu.VMEM((3, cols, chans), BF16),
        pltpu.VMEM((3, cols, chans), BF16),
        pltpu.VMEM((3, rows, chans), BF16),
        pltpu.VMEM((3, rows, chans), BF16),
        pltpu.VMEM((4, 3, 16, chans), BF16),
        pltpu.SemaphoreType.DMA((8,)),
        pltpu.SemaphoreType.DMA((8,)),
    ]


class Halo:
    def __init__(self, nty, ntx, block, left, right, bufs):
        self.nty, self.ntx = nty, ntx
        self.ty, self.tx = lax.axis_index("ty"), lax.axis_index("tx")
        self.block, self.left, self.right = block, left, right
        self.bufs = bufs

    def there(self, dy, dx):
        ok = None
        for step, at, count in ((dy, self.ty, self.nty), (dx, self.tx, self.ntx)):
            if step:
                one = (at > 0) if step < 0 else (at < count - 1)
                ok = one if ok is None else jnp.logical_and(ok, one)
        return ok

    def greet(self, barrier):
        count = jnp.int32(0)
        for dy, dx in STEPS:
            ok = self.there(dy, dx)

            @pl.when(ok)
            def _(dy=dy, dx=dx):
                pl.semaphore_signal(
                    barrier, inc=1, device_id=(self.ty + dy, self.tx + dx), device_id_type=MESH
                )

            count = count + jnp.where(ok, 1, 0)
        return count

    def copy(self, index):
        dy, dx = STEPS[index]
        top, bottom, left, right, corner, send, recv = self.bufs
        rows = self.block.shape[0]
        src, dst = (
            (self.block.at[0:3], bottom),
            (self.block.at[rows - 3 : rows], top),
            (self.left, right),
            (self.right, left),
            (self.left.at[:, 0:16], corner.at[3]),
            (self.right.at[:, 0:16], corner.at[2]),
            (self.left.at[:, rows - 16 : rows], corner.at[1]),
            (self.right.at[:, rows - 16 : rows], corner.at[0]),
        )[index]
        return pltpu.make_async_remote_copy(
            src_ref=src,
            dst_ref=dst,
            send_sem=send.at[index],
            recv_sem=recv.at[index],
            device_id=(self.ty + dy, self.tx + dx),
            device_id_type=MESH,
        )

    def start(self):
        for index, step in enumerate(STEPS):

            @pl.when(self.there(*step))
            def _(index=index):
                self.copy(index).start()

    def fill(self, work):
        rows, cols, chans = self.block.shape
        halves = chans // 128

        def zero(i, _):
            at = pl.multiple_of(i * PITCH, PITCH)
            work[pl.ds(at, PITCH), :] = jnp.zeros((PITCH, 128), F32)
            return 0

        for h in range(halves):
            lax.fori_loop(h * (rows + 6), h * (rows + 6) + 3, zero, 0)
            lax.fori_loop((h + 1) * (rows + 6) - 3, (h + 1) * (rows + 6), zero, 0)

        def row(i, _):
            for h in range(halves):
                at = pl.multiple_of((h * (rows + 6) + 3 + i) * PITCH, PITCH)
                work[pl.ds(at, 8), :] = jnp.zeros((8, 128), F32)
                work[pl.ds(at + 8, cols), :] = self.block[i, :, h * 128 : h * 128 + 128].astype(F32)
                work[pl.ds(at + 8 + cols, 8), :] = jnp.zeros((8, 128), F32)
            return 0

        lax.fori_loop(0, rows, row, 0)

    def finish(self, work):
        rows, cols, chans = self.block.shape
        halves = chans // 128
        top, bottom, left, right, corner, _, _ = self.bufs
        for index, (dy, dx) in enumerate(STEPS):

            @pl.when(self.there(-dy, -dx))
            def _(index=index):
                self.copy(index).wait_recv()

                for h in range(halves):
                    lanes = slice(h * 128, h * 128 + 128)
                    base = h * (rows + 6)
                    if index < 2:
                        first = 3 + rows if index == 0 else 0
                        src = bottom if index == 0 else top
                        for r in range(3):
                            work[pl.ds((base + first + r) * PITCH + 8, cols), :] = src[r, :, lanes].astype(F32)
                    elif index < 4:
                        first = 8 + cols if index == 2 else 5
                        src = right if index == 2 else left
                        for k in range(3):
                            for g in range(rows // 16):
                                vals = src[k, g * 16 : g * 16 + 16, lanes].astype(F32)
                                for s in range(2):
                                    at = (base + 3 + g * 16 + s * 8) * PITCH + first + k
                                    work[pl.ds(at, 8, stride=PITCH), :] = vals[s * 8 : s * 8 + 8]
                    else:
                        slot = 7 - index
                        low, near = slot < 2, slot % 2 == 0
                        for k in range(3):
                            vals = corner[slot, k, :, lanes].astype(F32)
                            for r in range(3):
                                row = base + (r if low else 3 + rows + r)
                                at = row * PITCH + (5 if near else 8 + cols) + k
                                pick = (13 + r) if low else r
                                work[pl.ds(at, 1), :] = vals[pick : pick + 1]

        for index, step in enumerate(STEPS):

            @pl.when(self.there(*step))
            def _(index=index):
                self.copy(index).wait_send()


def spot(t, rows, cols):
    per = (rows // 4) * (cols // 16)
    h = t // per
    rest = t % per
    r = (rest // (cols // 16)) * 4
    c = (rest % (cols // 16)) * 16
    at = pl.multiple_of((h * (rows + 6) + r) * PITCH + c, 16)
    return h, r, pl.multiple_of(c, 16), at


def conv_block(work, taps, h, at, flip):
    total = [None] * 4
    for b in range(7):
        lines = [work[pl.ds(at + r * PITCH + 5 + b, 16), :] for r in range(10)]
        for a in range(7):
            tap = a * 7 + b
            tap = 48 - tap if flip else tap
            weight = taps[pl.ds(h * 49 + tap, 1), :]
            for o in range(4):
                term = lines[o + a] * weight
                total[o] = term if total[o] is None else total[o] + term
    return total


def pre_kernel(nty, ntx, block, left, right, taps, bias, out, work, *bufs):
    rows, cols, chans = block.shape
    halo = Halo(nty, ntx, block, left, right, bufs)
    barrier = pltpu.get_barrier_semaphore()
    count = halo.greet(barrier)
    pl.semaphore_wait(barrier, count)
    halo.start()
    halo.fill(work)

    def block_at(half, r, c):
        at = pl.multiple_of((half * (rows + 6) + r) * PITCH + c, 16)
        total = conv_block(work, taps, half, at, False)
        for o in range(4):
            lanes = slice(half * 128, half * 128 + 128)
            out[r + o, pl.ds(c, 16), lanes] = total[o] + bias[pl.ds(half, 1), :]

    inner = cols // 16 - 2
    for half in range(chans // 128):

        def inside(t, _, half=half):
            block_at(half, (1 + t // inner) * 4, pl.multiple_of((1 + t % inner) * 16, 16))
            return 0

        lax.fori_loop(0, (rows // 4 - 2) * inner, inside, 0)
    halo.finish(work)
    for half in range(chans // 128):

        def edge(t, _, half=half):
            block_at(half, (1 + t // 2) * 4, pl.multiple_of((t % 2) * (cols - 16), 16))
            return 0

        def ends(t, _, half=half):
            wide = cols // 16
            block_at(half, (t // wide) * (rows - 4), pl.multiple_of((t % wide) * 16, 16))
            return 0

        lax.fori_loop(0, (rows // 4 - 2) * 2, edge, 0)
        lax.fori_loop(0, 2 * (cols // 16), ends, 0)


def post_kernel(
    nty, ntx, size, wide, factor, block, left, right, xblock_pad, cot, taps, sums_in,
    out, dw, expand, reduce, sums, dsum, work, dacc, ssend, srecv, gathered, dsend, drecv,
    s_send, s_recv, d_send, d_recv, *bufs,
):
    rows, cols, chans = block.shape
    halves = chans // 128
    halo = Halo(nty, ntx, block, left, right, bufs)
    ty, tx = halo.ty, halo.tx
    bits = [("ty", 1 << k) for k in range(nty.bit_length() - 1)]
    bits += [("tx", 1 << k) for k in range(ntx.bit_length() - 1)]
    nb = len(bits)

    def mine(k):
        axis, bit = bits[k]
        return ((ty if axis == "ty" else tx) // bit) % 2

    def partner(k):
        axis, bit = bits[k]
        step = bit - 2 * bit * mine(k)
        return (ty + step, tx) if axis == "ty" else (ty, tx + step)

    barrier = pltpu.get_barrier_semaphore()
    count = halo.greet(barrier)
    for k in range(nb):
        pl.semaphore_signal(barrier, inc=1, device_id=partner(k), device_id_type=MESH)
    pl.semaphore_wait(barrier, count + nb)
    halo.start()

    lows = [jnp.int32(0)]
    for k in range(nb):
        lows.append(lows[k] + mine(k) * (size >> (k + 1)))

    def by_chunk(length, fn):
        step = min(length, 128)

        def go(i, _):
            fn(pl.multiple_of(i * step, 16), step)
            return 0

        lax.fori_loop(0, length // step, go, 0)

    def rs_copy(k):
        length = size >> (k + 1)
        away = pl.multiple_of(lows[k] + (1 - mine(k)) * length, 16)
        return pltpu.make_async_remote_copy(
            src_ref=ssend.at[pl.ds(away, length)],
            dst_ref=srecv.at[pl.ds(size - 2 * length, length)],
            send_sem=s_send.at[k],
            recv_sem=s_recv.at[k],
            device_id=partner(k),
            device_id_type=MESH,
        )

    def rs_start(k):
        length = size >> (k + 1)
        away = lows[k] + (1 - mine(k)) * length
        source = sums_in if k == 0 else sums

        def cast(i, step):
            at = pl.multiple_of(away + i, 16)
            ssend[pl.ds(at, step), :] = source[pl.ds(at, step), :].astype(BF16)

        by_chunk(length, cast)
        rs_copy(k).start()

    def rs_end(k):
        length = size >> (k + 1)
        source = sums_in if k == 0 else sums
        rs_copy(k).wait()

        def add(i, step):
            at = pl.multiple_of(lows[k + 1] + i, 16)
            got = srecv[pl.ds(pl.multiple_of(size - 2 * length + i, 16), step), :]
            sums[pl.ds(at, step), :] = source[pl.ds(at, step), :] + got.astype(F32)

        by_chunk(length, add)

    def ag_copy(k):
        length = size >> (k + 1)
        at = pl.multiple_of(lows[k + 1], 16)
        return pltpu.make_async_remote_copy(
            src_ref=gathered.at[pl.ds(at, length)],
            dst_ref=gathered.at[pl.ds(at, length)],
            send_sem=s_send.at[nb + k],
            recv_sem=s_recv.at[nb + k],
            device_id=partner(k),
            device_id_type=MESH,
        )

    def ag_start(k):
        if k == nb - 1:
            length = size >> nb

            def cast(i, step):
                at = pl.multiple_of(lows[nb] + i, 16)
                gathered[pl.ds(at, step), :] = sums[pl.ds(at, step), :].astype(BF16)

            by_chunk(length, cast)
        ag_copy(k).start()

    def d_copy(k):
        return pltpu.make_async_remote_copy(
            src_ref=dsend.at[k],
            dst_ref=drecv.at[k],
            send_sem=d_send.at[k],
            recv_sem=d_recv.at[k],
            device_id=partner(k),
            device_id_type=MESH,
        )

    events = []
    for k in range(nb):
        events.append((functools.partial(rs_start, k), functools.partial(rs_end, k)))
    for k in reversed(range(nb)):
        events.append((functools.partial(ag_start, k), ag_copy(k).wait))
    d_events = [(d_copy(k).start, functools.partial(lambda k: d_end(k), k)) for k in range(nb)]

    def d_end(k):
        d_copy(k).wait()
        new = dsend[k] + drecv[k]
        if k + 1 < nb:
            dsend[k + 1] = new
        else:
            dsum[...] = new

    events[0][0]()
    at_event = [0, 0]

    def advance(upto, which, line):
        while at_event[which] < upto:
            e = at_event[which]
            line[e][1]()
            if e + 1 < len(line):
                line[e + 1][0]()
            at_event[which] += 1

    def due(count, done, over):
        return min(count, -(-count * done // over))

    halo.fill(work)
    dacc[...] = jnp.zeros_like(dacc)
    blocks = halves * (rows // 4) * (cols // 16)

    def grad_step(t, _):
        h, r, c, at = spot(t, rows, cols)
        mid = pl.multiple_of(at + 3 * PITCH + 8, 8)
        gs = [work[pl.ds(mid + o * PITCH, 16), :] for o in range(4)]
        for b in range(7):
            lines = [xblock_pad[pl.ds(at + q * PITCH + 5 + b, 16), :] for q in range(10)]
            for a in range(7):
                term = lines[a] * gs[0]
                for o in range(1, 4):
                    term = term + lines[o + a] * gs[o]
                slot = pl.multiple_of((h * 49 + a * 7 + b) * 8, 8)
                dacc[pl.ds(slot, 8), :] = dacc[pl.ds(slot, 8), :] + (term[:8] + term[8:])
        return 0

    def out_step(half, t, _):
        _, r, c, at = spot(t, rows, cols)
        total = conv_block(work, taps, half, at, True)
        for o in range(4):
            lanes = slice(half * 128, half * 128 + 128)
            res = total[o] + cot[r + o, pl.ds(c, 16), lanes].astype(F32)
            out[r + o, pl.ds(c, 16), lanes] = res.astype(BF16)
        return 0

    pieces = 6
    each = blocks // pieces
    for p in range(pieces):
        lax.fori_loop(p * each, (p + 1) * each, grad_step, 0)
        advance(due(len(events), p + 1, 2 * pieces - 1), 0, events)

    def fold(i, _):
        at = pl.multiple_of(i * 8, 8)
        dsend[0, pl.ds(i, 1), :] = jnp.sum(dacc[pl.ds(at, 8), :], axis=0, keepdims=True)
        return 0

    dsend[0, 96:104, :] = jnp.zeros((8, 128), F32)
    lax.fori_loop(0, halves * 49, fold, 0)
    d_events[0][0]()
    halo.finish(work)
    for p in range(pieces):
        lax.fori_loop(
            p * each, (p + 1) * each, functools.partial(out_step, p * halves // pieces), 0
        )
        advance(due(len(events), pieces + p + 1, 2 * pieces - 1), 0, events)
        advance(due(nb, p + 1, pieces - 1), 1, d_events)

    for k in range(wide):
        expand[:, k * 128 : (k + 1) * 128] = gathered[k * chans : (k + 1) * chans, :].astype(F32) * factor
        at = (wide + k) * chans
        part = gathered[at : at + chans, :].astype(F32) * factor
        reduce[k * 128 : (k + 1) * 128, :] = jnp.transpose(part)
    for h in range(halves):
        dw[:, h * 128 : (h + 1) * 128] = dsum[h * 49 : (h + 1) * 49, :] * factor


def strips(block):
    cols = block.shape[1]
    return (
        jnp.transpose(block[:, :3], (1, 0, 2)),
        jnp.transpose(block[:, cols - 3 :], (1, 0, 2)),
    )


def contract(left, right, ldim, rdim):
    return lax.dot_general(
        left, right, (((ldim,), (rdim,)), ((), ())), preferred_element_type=F32
    )


def mid_kernel(pre, cot, tissue, gain, shift, w_expand, b_expand, w_reduce, scale, grad, sums):
    rows, cols, chans = pre.shape
    hid = w_expand.shape[1]
    pixels = rows * cols
    turn = pl.program_id(0)

    @pl.when(turn == 0)
    def _():
        sums[...] = jnp.zeros_like(sums)

    masked = jnp.concatenate(
        [
            cot[:, k * TILE : (k + 1) * TILE, :].astype(F32) * tissue[turn, k].astype(F32)
            for k in range(cols // TILE)
        ],
        axis=1,
    ).reshape(pixels, chans)
    go_vals = (scale[...] * masked).astype(BF16)
    vals = pre[...].reshape(pixels, chans)
    center = vals - jnp.mean(vals, axis=-1, keepdims=True)
    rstd = lax.rsqrt(jnp.mean(center * center, axis=-1, keepdims=True) + 1e-06)
    nhat = center * rstd
    normed = (nhat * gain[...] + shift[...]).astype(BF16)
    go_t = jnp.transpose(go_vals)
    normed_t = jnp.transpose(normed)
    part = 256
    dnorm = None
    for k in range(hid // part):
        span = slice(k * part, (k + 1) * part)
        zvals = contract(normed, w_expand[:, span], 1, 0) + b_expand[:, span]
        cdf = 0.5 * (1.0 + lax.erf(zvals * 0.7071067811865476))
        hidden = (zvals * cdf).astype(BF16)
        slope = cdf + zvals * jnp.exp(-0.5 * zvals * zvals) * 0.3989422804014327
        dzvals = (contract(go_vals, w_reduce[span, :], 1, 1) * slope).astype(BF16)
        term = contract(dzvals, w_expand[:, span], 1, 1)
        dnorm = term if dnorm is None else dnorm + term
        to_expand = contract(normed_t, dzvals, 1, 0)
        to_reduce = contract(go_t, hidden, 1, 0)
        for j in range(part // 128):
            lanes = slice(j * 128, (j + 1) * 128)
            at = (k * (part // 128) + j) * chans
            sums[at : at + chans, :] += to_expand[:, lanes]
            at += hid // 128 * chans
            sums[at : at + chans, :] += to_reduce[:, lanes]
    dnorm = dnorm * gain[...]
    result = rstd * (
        dnorm
        - jnp.mean(dnorm, axis=-1, keepdims=True)
        - nhat * jnp.mean(dnorm * nhat, axis=-1, keepdims=True)
    )
    grad[...] = result.astype(BF16).reshape(rows, cols, chans)


def body(
    nty,
    ntx,
    block_input,
    cotangent,
    tissue,
    dw_weight,
    dw_bias,
    ln_gain,
    ln_bias,
    w_expand,
    b_expand,
    w_reduce,
    layer_scale,
):
    rows, cols, chans = block_input.shape
    hid = w_expand.shape[1]
    halves = chans // 128
    padded = halves * (rows + 6) * PITCH
    taps = jnp.transpose(dw_weight.reshape(49, halves, 128), (1, 0, 2)).reshape(halves * 49, 128)
    vmem = pl.BlockSpec(memory_space=pltpu.VMEM)
    flops = 49 * 2 * rows * cols * chans
    pre, xpad = pl.pallas_call(
        functools.partial(pre_kernel, nty, ntx),
        out_shape=(
            jax.ShapeDtypeStruct((rows, cols, chans), F32),
            jax.ShapeDtypeStruct((padded, 128), F32),
        ),
        in_specs=[vmem] * 5,
        out_specs=(vmem, vmem),
        scratch_shapes=halo_bufs(cols, rows, chans),
        compiler_params=pltpu.CompilerParams(
            collective_id=0, has_side_effects=True, vmem_limit_bytes=40 << 20
        ),
        cost_estimate=pl.CostEstimate(flops=flops, bytes_accessed=16 << 20, transcendentals=0),
        name="pre",
    )(block_input, *strips(block_input), taps, dw_bias.reshape(halves, 128))

    wide = hid // 128
    unit = nty * ntx * 16
    size = -(-2 * wide * chans // unit) * unit
    one = lambda array: pl.BlockSpec(array.shape, lambda i: (0,) * array.ndim)
    per_tile = pl.BlockSpec((TILE, cols, chans), lambda i: (i, 0, 0))
    whole = [
        ln_gain.reshape(1, chans),
        ln_bias.reshape(1, chans),
        w_expand,
        b_expand.reshape(1, hid),
        w_reduce,
        layer_scale.reshape(1, chans),
    ]
    grad_core, sums_in = pl.pallas_call(
        mid_kernel,
        grid=(rows // TILE,),
        out_shape=(
            jax.ShapeDtypeStruct((rows, cols, chans), BF16),
            jax.ShapeDtypeStruct((size, 128), F32),
        ),
        in_specs=[per_tile, per_tile, pl.BlockSpec(memory_space=pltpu.SMEM)]
        + [one(array) for array in whole],
        out_specs=(per_tile, pl.BlockSpec((size, 128), lambda i: (0, 0))),
        compiler_params=pltpu.CompilerParams(vmem_limit_bytes=44 << 20),
        cost_estimate=pl.CostEstimate(
            flops=10 * rows * cols * chans * hid,
            bytes_accessed=12 << 20,
            transcendentals=2 * rows * cols * hid,
        ),
        name="mid",
    )(pre, cotangent, tissue, *whole)

    factor = 1.0 / math.sqrt(rows * nty * cols * ntx)
    nb = (nty * ntx).bit_length() - 1
    return pl.pallas_call(
        functools.partial(post_kernel, nty, ntx, size, wide, factor),
        out_shape=(
            jax.ShapeDtypeStruct((rows, cols, chans), BF16),
            jax.ShapeDtypeStruct((49, chans), F32),
            jax.ShapeDtypeStruct((chans, hid), F32),
            jax.ShapeDtypeStruct((hid, chans), F32),
        ),
        in_specs=[vmem] * 7,
        out_specs=(vmem,) * 4,
        scratch_shapes=[
            pltpu.VMEM((size, 128), F32),
            pltpu.VMEM((104, 128), F32),
            pltpu.VMEM((padded, 128), F32),
            pltpu.VMEM((halves * 49 * 8, 128), F32),
            pltpu.VMEM((size, 128), BF16),
            pltpu.VMEM((size, 128), BF16),
            pltpu.VMEM((size, 128), BF16),
            pltpu.VMEM((nb, 104, 128), F32),
            pltpu.VMEM((nb, 104, 128), F32),
            pltpu.SemaphoreType.DMA((2 * nb,)),
            pltpu.SemaphoreType.DMA((2 * nb,)),
            pltpu.SemaphoreType.DMA((nb,)),
            pltpu.SemaphoreType.DMA((nb,)),
        ]
        + halo_bufs(cols, rows, chans),
        compiler_params=pltpu.CompilerParams(
            collective_id=1, has_side_effects=True, vmem_limit_bytes=50 << 20
        ),
        cost_estimate=pl.CostEstimate(flops=2 * flops, bytes_accessed=24 << 20, transcendentals=0),
        name="post",
    )(grad_core, *strips(grad_core), xpad, cotangent, taps, sums_in)


def solution(mesh):
    placed = (P("ty", "tx", None), P("ty", "tx", None), P("ty", "tx")) + (P(),) * 8
    return jax.shard_map(
        functools.partial(body, mesh.shape["ty"], mesh.shape["tx"]),
        mesh=mesh,
        in_specs=placed,
        out_specs=(P("ty", "tx", None), P(), P(), P()),
        check_vma=False,
    )
```

```python
import functools
import math

import jax
import jax.numpy as jnp
from jax import lax
from jax.experimental import pallas as pl
from jax.experimental.pallas import tpu as pltpu
from jax.sharding import PartitionSpec as P

TILE = 16
MESH = pl.DeviceIdType.MESH
F32, BF16 = jnp.float32, jnp.bfloat16
STEPS = ((-1, 0), (1, 0), (0, -1), (0, 1), (-1, -1), (-1, 1), (1, -1), (1, 1))
PITCH = 64


def halo_bufs(cols, rows, chans):
    return [
        pltpu.VMEM((3, cols, chans), BF16),
        pltpu.VMEM((3, cols, chans), BF16),
        pltpu.VMEM((3, rows, chans), BF16),
        pltpu.VMEM((3, rows, chans), BF16),
        pltpu.VMEM((4, 3, 16, chans), BF16),
        pltpu.SemaphoreType.DMA((8,)),
        pltpu.SemaphoreType.DMA((8,)),
    ]


class Halo:
    def __init__(self, nty, ntx, block, left, right, bufs):
        self.nty, self.ntx = nty, ntx
        self.ty, self.tx = lax.axis_index("ty"), lax.axis_index("tx")
        self.block, self.left, self.right = block, left, right
        self.bufs = bufs

    def there(self, dy, dx):
        ok = None
        for step, at, count in ((dy, self.ty, self.nty), (dx, self.tx, self.ntx)):
            if step:
                one = (at > 0) if step < 0 else (at < count - 1)
                ok = one if ok is None else jnp.logical_and(ok, one)
        return ok

    def greet(self, barrier):
        count = jnp.int32(0)
        for dy, dx in STEPS:
            ok = self.there(dy, dx)

            @pl.when(ok)
            def _(dy=dy, dx=dx):
                pl.semaphore_signal(
                    barrier, inc=1, device_id=(self.ty + dy, self.tx + dx), device_id_type=MESH
                )

            count = count + jnp.where(ok, 1, 0)
        return count

    def copy(self, index):
        dy, dx = STEPS[index]
        top, bottom, left, right, corner, send, recv = self.bufs
        rows = self.block.shape[0]
        src, dst = (
            (self.block.at[0:3], bottom),
            (self.block.at[rows - 3 : rows], top),
            (self.left, right),
            (self.right, left),
            (self.left.at[:, 0:16], corner.at[3]),
            (self.right.at[:, 0:16], corner.at[2]),
            (self.left.at[:, rows - 16 : rows], corner.at[1]),
            (self.right.at[:, rows - 16 : rows], corner.at[0]),
        )[index]
        return pltpu.make_async_remote_copy(
            src_ref=src,
            dst_ref=dst,
            send_sem=send.at[index],
            recv_sem=recv.at[index],
            device_id=(self.ty + dy, self.tx + dx),
            device_id_type=MESH,
        )

    def start(self):
        for index, step in enumerate(STEPS):

            @pl.when(self.there(*step))
            def _(index=index):
                self.copy(index).start()

    def fill(self, work):
        rows, cols, chans = self.block.shape
        halves = chans // 128

        def zero(i, _):
            at = pl.multiple_of(i * PITCH, PITCH)
            work[pl.ds(at, PITCH), :] = jnp.zeros((PITCH, 128), F32)
            return 0

        for h in range(halves):
            lax.fori_loop(h * (rows + 6), h * (rows + 6) + 3, zero, 0)
            lax.fori_loop((h + 1) * (rows + 6) - 3, (h + 1) * (rows + 6), zero, 0)

        def row(i, _):
            for h in range(halves):
                at = pl.multiple_of((h * (rows + 6) + 3 + i) * PITCH, PITCH)
                work[pl.ds(at, 8), :] = jnp.zeros((8, 128), F32)
                work[pl.ds(at + 8, cols), :] = self.block[i, :, h * 128 : h * 128 + 128].astype(F32)
                work[pl.ds(at + 8 + cols, 8), :] = jnp.zeros((8, 128), F32)
            return 0

        lax.fori_loop(0, rows, row, 0)

    def finish(self, work):
        rows, cols, chans = self.block.shape
        halves = chans // 128
        top, bottom, left, right, corner, _, _ = self.bufs
        for index, (dy, dx) in enumerate(STEPS):

            @pl.when(self.there(-dy, -dx))
            def _(index=index):
                self.copy(index).wait_recv()

                for h in range(halves):
                    lanes = slice(h * 128, h * 128 + 128)
                    base = h * (rows + 6)
                    if index < 2:
                        first = 3 + rows if index == 0 else 0
                        src = bottom if index == 0 else top
                        for r in range(3):
                            work[pl.ds((base + first + r) * PITCH + 8, cols), :] = src[r, :, lanes].astype(F32)
                    elif index < 4:
                        first = 8 + cols if index == 2 else 5
                        src = right if index == 2 else left
                        for k in range(3):
                            for g in range(rows // 16):
                                vals = src[k, g * 16 : g * 16 + 16, lanes].astype(F32)
                                for s in range(2):
                                    at = (base + 3 + g * 16 + s * 8) * PITCH + first + k
                                    work[pl.ds(at, 8, stride=PITCH), :] = vals[s * 8 : s * 8 + 8]
                    else:
                        slot = 7 - index
                        low, near = slot < 2, slot % 2 == 0
                        for k in range(3):
                            vals = corner[slot, k, :, lanes].astype(F32)
                            for r in range(3):
                                row = base + (r if low else 3 + rows + r)
                                at = row * PITCH + (5 if near else 8 + cols) + k
                                pick = (13 + r) if low else r
                                work[pl.ds(at, 1), :] = vals[pick : pick + 1]

        for index, step in enumerate(STEPS):

            @pl.when(self.there(*step))
            def _(index=index):
                self.copy(index).wait_send()


def spot(t, rows, cols):
    per = (rows // 4) * (cols // 16)
    h = t // per
    rest = t % per
    r = (rest // (cols // 16)) * 4
    c = (rest % (cols // 16)) * 16
    at = pl.multiple_of((h * (rows + 6) + r) * PITCH + c, 16)
    return h, r, pl.multiple_of(c, 16), at


def conv_block(work, taps, h, at, flip):
    total = [None] * 4
    for b in range(7):
        lines = [work[pl.ds(at + r * PITCH + 5 + b, 16), :] for r in range(10)]
        for a in range(7):
            tap = a * 7 + b
            tap = 48 - tap if flip else tap
            weight = taps[pl.ds(h * 49 + tap, 1), :]
            for o in range(4):
                term = lines[o + a] * weight
                total[o] = term if total[o] is None else total[o] + term
    return total


def pre_kernel(nty, ntx, block, left, right, taps, bias, out, work, *bufs):
    rows, cols, chans = block.shape
    halo = Halo(nty, ntx, block, left, right, bufs)
    barrier = pltpu.get_barrier_semaphore()
    count = halo.greet(barrier)
    pl.semaphore_wait(barrier, count)
    halo.start()
    halo.fill(work)

    def block_at(half, r, c):
        at = pl.multiple_of((half * (rows + 6) + r) * PITCH + c, 16)
        total = conv_block(work, taps, half, at, False)
        for o in range(4):
            lanes = slice(half * 128, half * 128 + 128)
            out[r + o, pl.ds(c, 16), lanes] = total[o] + bias[pl.ds(half, 1), :]

    inner = cols // 16 - 2
    for half in range(chans // 128):

        def inside(t, _, half=half):
            block_at(half, (1 + t // inner) * 4, pl.multiple_of((1 + t % inner) * 16, 16))
            return 0

        lax.fori_loop(0, (rows // 4 - 2) * inner, inside, 0)
    halo.finish(work)
    for half in range(chans // 128):

        def edge(t, _, half=half):
            block_at(half, (1 + t // 2) * 4, pl.multiple_of((t % 2) * (cols - 16), 16))
            return 0

        def ends(t, _, half=half):
            wide = cols // 16
            block_at(half, (t // wide) * (rows - 4), pl.multiple_of((t % wide) * 16, 16))
            return 0

        lax.fori_loop(0, (rows // 4 - 2) * 2, edge, 0)
        lax.fori_loop(0, 2 * (cols // 16), ends, 0)


def post_kernel(
    nty, ntx, size, wide, factor, block, left, right, xblock_pad, cot, taps, sums_in,
    out, dw, expand, reduce, sums, dsum, work, dacc, ssend, srecv, gathered, dsend, drecv,
    s_send, s_recv, d_send, d_recv, *bufs,
):
    rows, cols, chans = block.shape
    halves = chans // 128
    halo = Halo(nty, ntx, block, left, right, bufs)
    ty, tx = halo.ty, halo.tx
    bits = [("ty", 1 << k) for k in range(nty.bit_length() - 1)]
    bits += [("tx", 1 << k) for k in range(ntx.bit_length() - 1)]
    nb = len(bits)

    def mine(k):
        axis, bit = bits[k]
        return ((ty if axis == "ty" else tx) // bit) % 2

    def partner(k):
        axis, bit = bits[k]
        step = bit - 2 * bit * mine(k)
        return (ty + step, tx) if axis == "ty" else (ty, tx + step)

    barrier = pltpu.get_barrier_semaphore()
    count = halo.greet(barrier)
    for k in range(nb):
        pl.semaphore_signal(barrier, inc=1, device_id=partner(k), device_id_type=MESH)
    pl.semaphore_wait(barrier, count + nb)
    halo.start()


    def by_chunk(length, fn):
        step = min(length, 128)

        def go(i, _):
            fn(pl.multiple_of(i * step, 16), step)
            return 0

        lax.fori_loop(0, length // step, go, 0)

    def chain(base, size, order, sem):
        lows = [jnp.int32(base)]
        for k in range(nb):
            lows.append(lows[k] + mine(order[k]) * (size >> (k + 1)))

        def rs_copy(k):
            length = size >> (k + 1)
            away = pl.multiple_of(lows[k] + (1 - mine(order[k])) * length, 16)
            return pltpu.make_async_remote_copy(
                src_ref=ssend.at[pl.ds(away, length)],
                dst_ref=srecv.at[pl.ds(base + size - 2 * length, length)],
                send_sem=s_send.at[sem + k],
                recv_sem=s_recv.at[sem + k],
                device_id=partner(order[k]),
                device_id_type=MESH,
            )

        def rs_start(k):
            length = size >> (k + 1)
            away = lows[k] + (1 - mine(order[k])) * length
            source = sums_in if k == 0 else sums

            def cast(i, step):
                at = pl.multiple_of(away + i, 16)
                ssend[pl.ds(at, step), :] = source[pl.ds(at, step), :].astype(BF16)

            by_chunk(length, cast)
            rs_copy(k).start()

        def rs_end(k):
            length = size >> (k + 1)
            source = sums_in if k == 0 else sums
            rs_copy(k).wait()

            def add(i, step):
                at = pl.multiple_of(lows[k + 1] + i, 16)
                got = srecv[pl.ds(pl.multiple_of(base + size - 2 * length + i, 16), step), :]
                sums[pl.ds(at, step), :] = source[pl.ds(at, step), :] + got.astype(F32)

            by_chunk(length, add)

        def ag_copy(k):
            length = size >> (k + 1)
            at = pl.multiple_of(lows[k + 1], 16)
            return pltpu.make_async_remote_copy(
                src_ref=gathered.at[pl.ds(at, length)],
                dst_ref=gathered.at[pl.ds(at, length)],
                send_sem=s_send.at[sem + nb + k],
                recv_sem=s_recv.at[sem + nb + k],
                device_id=partner(order[k]),
                device_id_type=MESH,
            )

        def ag_start(k):
            if k == nb - 1:
                length = size >> nb

                def cast(i, step):
                    at = pl.multiple_of(lows[nb] + i, 16)
                    gathered[pl.ds(at, step), :] = sums[pl.ds(at, step), :].astype(BF16)

                by_chunk(length, cast)
            ag_copy(k).start()

        events = []
        for k in range(nb):
            events.append((functools.partial(rs_start, k), functools.partial(rs_end, k)))
        for k in reversed(range(nb)):
            events.append((functools.partial(ag_start, k), ag_copy(k).wait))
        return events

    def d_copy(k):
        return pltpu.make_async_remote_copy(
            src_ref=dsend.at[k],
            dst_ref=drecv.at[k],
            send_sem=d_send.at[k],
            recv_sem=d_recv.at[k],
            device_id=partner(k),
            device_id_type=MESH,
        )

    first = list(range(nb))
    second = first[:1] + first[1:3][::-1] + first[3:]
    events = [
        (functools.partial(both, one[0], two[0]), functools.partial(both, one[1], two[1]))
        for one, two in zip(
            chain(0, size // 2, first, 0), chain(size // 2, size // 2, second, 2 * nb)
        )
    ]
    d_events = [(d_copy(k).start, functools.partial(lambda k: d_end(k), k)) for k in range(nb)]

    def d_end(k):
        d_copy(k).wait()
        new = dsend[k] + drecv[k]
        if k + 1 < nb:
            dsend[k + 1] = new
        else:
            dsum[...] = new

    events[0][0]()
    at_event = [0, 0]

    def advance(upto, which, line):
        while at_event[which] < upto:
            e = at_event[which]
            line[e][1]()
            if e + 1 < len(line):
                line[e + 1][0]()
            at_event[which] += 1

    def due(count, done, over):
        return min(count, -(-count * done // over))

    halo.fill(work)
    dacc[...] = jnp.zeros_like(dacc)
    blocks = halves * (rows // 4) * (cols // 16)

    def grad_step(t, _):
        h, r, c, at = spot(t, rows, cols)
        mid = pl.multiple_of(at + 3 * PITCH + 8, 8)
        gs = [work[pl.ds(mid + o * PITCH, 16), :] for o in range(4)]
        for b in range(7):
            lines = [xblock_pad[pl.ds(at + q * PITCH + 5 + b, 16), :] for q in range(10)]
            for a in range(7):
                term = lines[a] * gs[0]
                for o in range(1, 4):
                    term = term + lines[o + a] * gs[o]
                slot = pl.multiple_of((h * 49 + a * 7 + b) * 8, 8)
                dacc[pl.ds(slot, 8), :] = dacc[pl.ds(slot, 8), :] + (term[:8] + term[8:])
        return 0

    def out_step(half, t, _):
        _, r, c, at = spot(t, rows, cols)
        total = conv_block(work, taps, half, at, True)
        for o in range(4):
            lanes = slice(half * 128, half * 128 + 128)
            res = total[o] + cot[r + o, pl.ds(c, 16), lanes].astype(F32)
            out[r + o, pl.ds(c, 16), lanes] = res.astype(BF16)
        return 0

    pieces = 6
    each = blocks // pieces
    for p in range(pieces):
        lax.fori_loop(p * each, (p + 1) * each, grad_step, 0)
        advance(due(len(events), p + 1, 2 * pieces - 1), 0, events)

    def fold(i, _):
        at = pl.multiple_of(i * 8, 8)
        dsend[0, pl.ds(i, 1), :] = jnp.sum(dacc[pl.ds(at, 8), :], axis=0, keepdims=True)
        return 0

    dsend[0, 96:104, :] = jnp.zeros((8, 128), F32)
    lax.fori_loop(0, halves * 49, fold, 0)
    d_events[0][0]()
    halo.finish(work)
    for p in range(pieces):
        lax.fori_loop(
            p * each, (p + 1) * each, functools.partial(out_step, p * halves // pieces), 0
        )
        advance(due(len(events), pieces + p + 1, 2 * pieces - 1), 0, events)
        advance(due(nb, p + 1, pieces - 1), 1, d_events)

    for k in range(wide):
        expand[:, k * 128 : (k + 1) * 128] = gathered[k * chans : (k + 1) * chans, :].astype(F32) * factor
        at = (wide + k) * chans
        part = gathered[at : at + chans, :].astype(F32) * factor
        reduce[k * 128 : (k + 1) * 128, :] = jnp.transpose(part)
    for h in range(halves):
        dw[:, h * 128 : (h + 1) * 128] = dsum[h * 49 : (h + 1) * 49, :] * factor


def both(one, two):
    one()
    two()


def strips(block):
    cols = block.shape[1]
    return (
        jnp.transpose(block[:, :3], (1, 0, 2)),
        jnp.transpose(block[:, cols - 3 :], (1, 0, 2)),
    )


def contract(left, right, ldim, rdim):
    return lax.dot_general(
        left, right, (((ldim,), (rdim,)), ((), ())), preferred_element_type=F32
    )


def mid_kernel(pre, cot, tissue, gain, shift, w_expand, b_expand, w_reduce, scale, grad, sums):
    rows, cols, chans = pre.shape
    hid = w_expand.shape[1]
    pixels = rows * cols
    turn = pl.program_id(0)

    @pl.when(turn == 0)
    def _():
        sums[...] = jnp.zeros_like(sums)

    masked = jnp.concatenate(
        [
            cot[:, k * TILE : (k + 1) * TILE, :].astype(F32) * tissue[turn, k].astype(F32)
            for k in range(cols // TILE)
        ],
        axis=1,
    ).reshape(pixels, chans)
    go_vals = (scale[...] * masked).astype(BF16)
    vals = pre[...].reshape(pixels, chans)
    center = vals - jnp.mean(vals, axis=-1, keepdims=True)
    rstd = lax.rsqrt(jnp.mean(center * center, axis=-1, keepdims=True) + 1e-06)
    nhat = center * rstd
    normed = (nhat * gain[...] + shift[...]).astype(BF16)
    go_t = jnp.transpose(go_vals)
    normed_t = jnp.transpose(normed)
    part = 256
    dnorm = None
    for k in range(hid // part):
        span = slice(k * part, (k + 1) * part)
        zvals = contract(normed, w_expand[:, span], 1, 0) + b_expand[:, span]
        cdf = 0.5 * (1.0 + lax.erf(zvals * 0.7071067811865476))
        hidden = (zvals * cdf).astype(BF16)
        slope = cdf + zvals * jnp.exp(-0.5 * zvals * zvals) * 0.3989422804014327
        dzvals = (contract(go_vals, w_reduce[span, :], 1, 1) * slope).astype(BF16)
        term = contract(dzvals, w_expand[:, span], 1, 1)
        dnorm = term if dnorm is None else dnorm + term
        to_expand = contract(normed_t, dzvals, 1, 0)
        to_reduce = contract(go_t, hidden, 1, 0)
        for j in range(part // 128):
            lanes = slice(j * 128, (j + 1) * 128)
            at = (k * (part // 128) + j) * chans
            sums[at : at + chans, :] += to_expand[:, lanes]
            at += hid // 128 * chans
            sums[at : at + chans, :] += to_reduce[:, lanes]
    dnorm = dnorm * gain[...]
    result = rstd * (
        dnorm
        - jnp.mean(dnorm, axis=-1, keepdims=True)
        - nhat * jnp.mean(dnorm * nhat, axis=-1, keepdims=True)
    )
    grad[...] = result.astype(BF16).reshape(rows, cols, chans)


def body(
    nty,
    ntx,
    block_input,
    cotangent,
    tissue,
    dw_weight,
    dw_bias,
    ln_gain,
    ln_bias,
    w_expand,
    b_expand,
    w_reduce,
    layer_scale,
):
    rows, cols, chans = block_input.shape
    hid = w_expand.shape[1]
    halves = chans // 128
    padded = halves * (rows + 6) * PITCH
    taps = jnp.transpose(dw_weight.reshape(49, halves, 128), (1, 0, 2)).reshape(halves * 49, 128)
    vmem = pl.BlockSpec(memory_space=pltpu.VMEM)
    flops = 49 * 2 * rows * cols * chans
    pre, xpad = pl.pallas_call(
        functools.partial(pre_kernel, nty, ntx),
        out_shape=(
            jax.ShapeDtypeStruct((rows, cols, chans), F32),
            jax.ShapeDtypeStruct((padded, 128), F32),
        ),
        in_specs=[vmem] * 5,
        out_specs=(vmem, vmem),
        scratch_shapes=halo_bufs(cols, rows, chans),
        compiler_params=pltpu.CompilerParams(
            collective_id=0, has_side_effects=True, vmem_limit_bytes=40 << 20
        ),
        cost_estimate=pl.CostEstimate(flops=flops, bytes_accessed=16 << 20, transcendentals=0),
        name="pre",
    )(block_input, *strips(block_input), taps, dw_bias.reshape(halves, 128))

    wide = hid // 128
    unit = nty * ntx * 32
    size = -(-2 * wide * chans // unit) * unit
    one = lambda array: pl.BlockSpec(array.shape, lambda i: (0,) * array.ndim)
    per_tile = pl.BlockSpec((TILE, cols, chans), lambda i: (i, 0, 0))
    whole = [
        ln_gain.reshape(1, chans),
        ln_bias.reshape(1, chans),
        w_expand,
        b_expand.reshape(1, hid),
        w_reduce,
        layer_scale.reshape(1, chans),
    ]
    grad_core, sums_in = pl.pallas_call(
        mid_kernel,
        grid=(rows // TILE,),
        out_shape=(
            jax.ShapeDtypeStruct((rows, cols, chans), BF16),
            jax.ShapeDtypeStruct((size, 128), F32),
        ),
        in_specs=[per_tile, per_tile, pl.BlockSpec(memory_space=pltpu.SMEM)]
        + [one(array) for array in whole],
        out_specs=(per_tile, pl.BlockSpec((size, 128), lambda i: (0, 0))),
        compiler_params=pltpu.CompilerParams(vmem_limit_bytes=44 << 20),
        cost_estimate=pl.CostEstimate(
            flops=10 * rows * cols * chans * hid,
            bytes_accessed=12 << 20,
            transcendentals=2 * rows * cols * hid,
        ),
        name="mid",
    )(pre, cotangent, tissue, *whole)

    factor = 1.0 / math.sqrt(rows * nty * cols * ntx)
    nb = (nty * ntx).bit_length() - 1
    return pl.pallas_call(
        functools.partial(post_kernel, nty, ntx, size, wide, factor),
        out_shape=(
            jax.ShapeDtypeStruct((rows, cols, chans), BF16),
            jax.ShapeDtypeStruct((49, chans), F32),
            jax.ShapeDtypeStruct((chans, hid), F32),
            jax.ShapeDtypeStruct((hid, chans), F32),
        ),
        in_specs=[vmem] * 7,
        out_specs=(vmem,) * 4,
        scratch_shapes=[
            pltpu.VMEM((size, 128), F32),
            pltpu.VMEM((104, 128), F32),
            pltpu.VMEM((padded, 128), F32),
            pltpu.VMEM((halves * 49 * 8, 128), F32),
            pltpu.VMEM((size, 128), BF16),
            pltpu.VMEM((size, 128), BF16),
            pltpu.VMEM((size, 128), BF16),
            pltpu.VMEM((nb, 104, 128), F32),
            pltpu.VMEM((nb, 104, 128), F32),
            pltpu.SemaphoreType.DMA((4 * nb,)),
            pltpu.SemaphoreType.DMA((4 * nb,)),
            pltpu.SemaphoreType.DMA((nb,)),
            pltpu.SemaphoreType.DMA((nb,)),
        ]
        + halo_bufs(cols, rows, chans),
        compiler_params=pltpu.CompilerParams(
            collective_id=1, has_side_effects=True, vmem_limit_bytes=50 << 20
        ),
        cost_estimate=pl.CostEstimate(flops=2 * flops, bytes_accessed=24 << 20, transcendentals=0),
        name="post",
    )(grad_core, *strips(grad_core), xpad, cotangent, taps, sums_in)


def solution(mesh):
    placed = (P("ty", "tx", None), P("ty", "tx", None), P("ty", "tx")) + (P(),) * 8
    return jax.shard_map(
        functools.partial(body, mesh.shape["ty"], mesh.shape["tx"]),
        mesh=mesh,
        in_specs=placed,
        out_specs=(P("ty", "tx", None), P(), P(), P()),
        check_vma=False,
    )
```

```python
import functools
import math

import jax
import jax.numpy as jnp
from jax import lax
from jax.experimental import pallas as pl
from jax.experimental.pallas import tpu as pltpu
from jax.sharding import PartitionSpec as P

TILE = 16
MESH = pl.DeviceIdType.MESH
F32, BF16 = jnp.float32, jnp.bfloat16
STEPS = ((-1, 0), (1, 0), (0, -1), (0, 1), (-1, -1), (-1, 1), (1, -1), (1, 1))
PITCH = 64


def halo_bufs(cols, rows, chans):
    return [
        pltpu.VMEM((3, cols, chans), BF16),
        pltpu.VMEM((3, cols, chans), BF16),
        pltpu.VMEM((3, rows, chans), BF16),
        pltpu.VMEM((3, rows, chans), BF16),
        pltpu.VMEM((4, 3, 16, chans), BF16),
        pltpu.SemaphoreType.DMA((8,)),
        pltpu.SemaphoreType.DMA((8,)),
    ]


class Halo:
    def __init__(self, nty, ntx, block, left, right, bufs):
        self.nty, self.ntx = nty, ntx
        self.ty, self.tx = lax.axis_index("ty"), lax.axis_index("tx")
        self.block, self.left, self.right = block, left, right
        self.bufs = bufs

    def there(self, dy, dx):
        ok = None
        for step, at, count in ((dy, self.ty, self.nty), (dx, self.tx, self.ntx)):
            if step:
                one = (at > 0) if step < 0 else (at < count - 1)
                ok = one if ok is None else jnp.logical_and(ok, one)
        return ok

    def greet(self, barrier):
        count = jnp.int32(0)
        for dy, dx in STEPS:
            ok = self.there(dy, dx)

            @pl.when(ok)
            def _(dy=dy, dx=dx):
                pl.semaphore_signal(
                    barrier, inc=1, device_id=(self.ty + dy, self.tx + dx), device_id_type=MESH
                )

            count = count + jnp.where(ok, 1, 0)
        return count

    def copy(self, index):
        dy, dx = STEPS[index]
        top, bottom, left, right, corner, send, recv = self.bufs
        rows = self.block.shape[0]
        src, dst = (
            (self.block.at[0:3], bottom),
            (self.block.at[rows - 3 : rows], top),
            (self.left, right),
            (self.right, left),
            (self.left.at[:, 0:16], corner.at[3]),
            (self.right.at[:, 0:16], corner.at[2]),
            (self.left.at[:, rows - 16 : rows], corner.at[1]),
            (self.right.at[:, rows - 16 : rows], corner.at[0]),
        )[index]
        return pltpu.make_async_remote_copy(
            src_ref=src,
            dst_ref=dst,
            send_sem=send.at[index],
            recv_sem=recv.at[index],
            device_id=(self.ty + dy, self.tx + dx),
            device_id_type=MESH,
        )

    def start(self):
        for index, step in enumerate(STEPS):

            @pl.when(self.there(*step))
            def _(index=index):
                self.copy(index).start()

    def fill(self, work):
        rows, cols, chans = self.block.shape
        halves = chans // 128

        def zero(i, _):
            at = pl.multiple_of(i * PITCH, PITCH)
            work[pl.ds(at, PITCH), :] = jnp.zeros((PITCH, 128), F32)
            return 0

        for h in range(halves):
            lax.fori_loop(h * (rows + 6), h * (rows + 6) + 3, zero, 0)
            lax.fori_loop((h + 1) * (rows + 6) - 3, (h + 1) * (rows + 6), zero, 0)

        def row(i, _):
            for h in range(halves):
                at = pl.multiple_of((h * (rows + 6) + 3 + i) * PITCH, PITCH)
                work[pl.ds(at, 8), :] = jnp.zeros((8, 128), F32)
                work[pl.ds(at + 8, cols), :] = self.block[i, :, h * 128 : h * 128 + 128].astype(F32)
                work[pl.ds(at + 8 + cols, 8), :] = jnp.zeros((8, 128), F32)
            return 0

        lax.fori_loop(0, rows, row, 0)

    def finish(self, work):
        rows, cols, chans = self.block.shape
        halves = chans // 128
        top, bottom, left, right, corner, _, _ = self.bufs
        for index, (dy, dx) in enumerate(STEPS):

            @pl.when(self.there(-dy, -dx))
            def _(index=index):
                self.copy(index).wait_recv()

                for h in range(halves):
                    lanes = slice(h * 128, h * 128 + 128)
                    base = h * (rows + 6)
                    if index < 2:
                        first = 3 + rows if index == 0 else 0
                        src = bottom if index == 0 else top
                        for r in range(3):
                            work[pl.ds((base + first + r) * PITCH + 8, cols), :] = src[r, :, lanes].astype(F32)
                    elif index < 4:
                        first = 8 + cols if index == 2 else 5
                        src = right if index == 2 else left
                        for k in range(3):
                            for g in range(rows // 16):
                                vals = src[k, g * 16 : g * 16 + 16, lanes].astype(F32)
                                for s in range(2):
                                    at = (base + 3 + g * 16 + s * 8) * PITCH + first + k
                                    work[pl.ds(at, 8, stride=PITCH), :] = vals[s * 8 : s * 8 + 8]
                    else:
                        slot = 7 - index
                        low, near = slot < 2, slot % 2 == 0
                        for k in range(3):
                            vals = corner[slot, k, :, lanes].astype(F32)
                            for r in range(3):
                                row = base + (r if low else 3 + rows + r)
                                at = row * PITCH + (5 if near else 8 + cols) + k
                                pick = (13 + r) if low else r
                                work[pl.ds(at, 1), :] = vals[pick : pick + 1]

        for index, step in enumerate(STEPS):

            @pl.when(self.there(*step))
            def _(index=index):
                self.copy(index).wait_send()


def spot(t, rows, cols):
    per = (rows // 4) * (cols // 16)
    h = t // per
    rest = t % per
    r = (rest // (cols // 16)) * 4
    c = (rest % (cols // 16)) * 16
    at = pl.multiple_of((h * (rows + 6) + r) * PITCH + c, 16)
    return h, r, pl.multiple_of(c, 16), at


def conv_block(work, taps, h, at, flip):
    total = [None] * 4
    for b in range(7):
        lines = [work[pl.ds(at + r * PITCH + 5 + b, 16), :] for r in range(10)]
        for a in range(7):
            tap = a * 7 + b
            tap = 48 - tap if flip else tap
            weight = taps[pl.ds(h * 49 + tap, 1), :]
            for o in range(4):
                term = lines[o + a] * weight
                total[o] = term if total[o] is None else total[o] + term
    return total


def pre_kernel(nty, ntx, block, left, right, taps, bias, out, work, *bufs):
    rows, cols, chans = block.shape
    halo = Halo(nty, ntx, block, left, right, bufs)
    barrier = pltpu.get_barrier_semaphore()
    count = halo.greet(barrier)
    pl.semaphore_wait(barrier, count)
    halo.start()
    halo.fill(work)

    def block_at(half, r, c):
        at = pl.multiple_of((half * (rows + 6) + r) * PITCH + c, 16)
        total = conv_block(work, taps, half, at, False)
        for o in range(4):
            lanes = slice(half * 128, half * 128 + 128)
            out[r + o, pl.ds(c, 16), lanes] = total[o] + bias[pl.ds(half, 1), :]

    inner = cols // 16 - 2
    for half in range(chans // 128):

        def inside(t, _, half=half):
            block_at(half, (1 + t // inner) * 4, pl.multiple_of((1 + t % inner) * 16, 16))
            return 0

        lax.fori_loop(0, (rows // 4 - 2) * inner, inside, 0)
    halo.finish(work)
    for half in range(chans // 128):

        def edge(t, _, half=half):
            block_at(half, (1 + t // 2) * 4, pl.multiple_of((t % 2) * (cols - 16), 16))
            return 0

        def ends(t, _, half=half):
            wide = cols // 16
            block_at(half, (t // wide) * (rows - 4), pl.multiple_of((t % wide) * 16, 16))
            return 0

        lax.fori_loop(0, (rows // 4 - 2) * 2, edge, 0)
        lax.fori_loop(0, 2 * (cols // 16), ends, 0)


def post_kernel(
    nty, ntx, size, wide, factor, block, left, right, xblock_pad, cot, taps, sums_in,
    out, dw, expand, reduce, sums, dsum, work, dacc, ssend, srecv, gathered, dsend, drecv,
    s_send, s_recv, d_send, d_recv, *bufs,
):
    rows, cols, chans = block.shape
    halves = chans // 128
    halo = Halo(nty, ntx, block, left, right, bufs)
    ty, tx = halo.ty, halo.tx
    bits = [("ty", 1 << k) for k in range(nty.bit_length() - 1)]
    bits += [("tx", 1 << k) for k in range(ntx.bit_length() - 1)]
    nb = len(bits)

    def mine(k):
        axis, bit = bits[k]
        return ((ty if axis == "ty" else tx) // bit) % 2

    def partner(k):
        axis, bit = bits[k]
        step = bit - 2 * bit * mine(k)
        return (ty + step, tx) if axis == "ty" else (ty, tx + step)

    barrier = pltpu.get_barrier_semaphore()
    count = halo.greet(barrier)
    for k in range(nb):
        pl.semaphore_signal(barrier, inc=1, device_id=partner(k), device_id_type=MESH)
    pl.semaphore_wait(barrier, count + nb)
    halo.start()


    def by_chunk(length, fn):
        step = min(length, 128)

        def go(i, _):
            fn(pl.multiple_of(i * step, 16), step)
            return 0

        lax.fori_loop(0, length // step, go, 0)

    def chain(base, size, order, sem):
        lows = [jnp.int32(base)]
        for k in range(nb):
            lows.append(lows[k] + mine(order[k]) * (size >> (k + 1)))

        def rs_copy(k):
            length = size >> (k + 1)
            away = pl.multiple_of(lows[k] + (1 - mine(order[k])) * length, 16)
            return pltpu.make_async_remote_copy(
                src_ref=ssend.at[pl.ds(away, length)],
                dst_ref=srecv.at[pl.ds(base + size - 2 * length, length)],
                send_sem=s_send.at[sem + k],
                recv_sem=s_recv.at[sem + k],
                device_id=partner(order[k]),
                device_id_type=MESH,
            )

        def rs_start(k):
            length = size >> (k + 1)
            away = lows[k] + (1 - mine(order[k])) * length
            source = sums_in if k == 0 else sums

            def cast(i, step):
                at = pl.multiple_of(away + i, 16)
                ssend[pl.ds(at, step), :] = source[pl.ds(at, step), :].astype(BF16)

            by_chunk(length, cast)
            rs_copy(k).start()

        def rs_end(k):
            length = size >> (k + 1)
            source = sums_in if k == 0 else sums
            rs_copy(k).wait()

            def add(i, step):
                at = pl.multiple_of(lows[k + 1] + i, 16)
                got = srecv[pl.ds(pl.multiple_of(base + size - 2 * length + i, 16), step), :]
                sums[pl.ds(at, step), :] = source[pl.ds(at, step), :] + got.astype(F32)

            by_chunk(length, add)

        def ag_copy(k):
            length = size >> (k + 1)
            at = pl.multiple_of(lows[k + 1], 16)
            return pltpu.make_async_remote_copy(
                src_ref=gathered.at[pl.ds(at, length)],
                dst_ref=gathered.at[pl.ds(at, length)],
                send_sem=s_send.at[sem + nb + k],
                recv_sem=s_recv.at[sem + nb + k],
                device_id=partner(order[k]),
                device_id_type=MESH,
            )

        def ag_start(k):
            if k == nb - 1:
                length = size >> nb

                def cast(i, step):
                    at = pl.multiple_of(lows[nb] + i, 16)
                    gathered[pl.ds(at, step), :] = sums[pl.ds(at, step), :].astype(BF16)

                by_chunk(length, cast)
            ag_copy(k).start()

        events = []
        for k in range(nb):
            events.append((functools.partial(rs_start, k), functools.partial(rs_end, k)))
        for k in reversed(range(nb)):
            events.append((functools.partial(ag_start, k), ag_copy(k).wait))
        return events

    def d_copy(k):
        return pltpu.make_async_remote_copy(
            src_ref=dsend.at[k],
            dst_ref=drecv.at[k],
            send_sem=d_send.at[k],
            recv_sem=d_recv.at[k],
            device_id=partner(k),
            device_id_type=MESH,
        )

    first = list(range(nb))
    second = first[:1] + first[1:3][::-1] + first[3:]
    events = [
        (functools.partial(both, one[0], two[0]), functools.partial(both, one[1], two[1]))
        for one, two in zip(
            chain(0, size // 2, first, 0), chain(size // 2, size // 2, second, 2 * nb)
        )
    ]
    d_events = [(d_copy(k).start, functools.partial(lambda k: d_end(k), k)) for k in range(nb)]

    def d_end(k):
        d_copy(k).wait()
        new = dsend[k] + drecv[k]
        if k + 1 < nb:
            dsend[k + 1] = new
        else:
            dsum[...] = new

    events[0][0]()
    at_event = [0, 0]

    def advance(upto, which, line):
        while at_event[which] < upto:
            e = at_event[which]
            line[e][1]()
            if e + 1 < len(line):
                line[e + 1][0]()
            at_event[which] += 1

    def due(count, done, over):
        return min(count, -(-count * done // over))

    halo.fill(work)
    dacc[...] = jnp.zeros_like(dacc)
    blocks = halves * (rows // 4) * (cols // 16)

    def grad_step(t, _):
        h, r, c, at = spot(t, rows, cols)
        mid = pl.multiple_of(at + 3 * PITCH + 8, 8)
        gs = [work[pl.ds(mid + o * PITCH, 16), :] for o in range(4)]
        for b in range(7):
            lines = [xblock_pad[pl.ds(at + q * PITCH + 5 + b, 16), :] for q in range(10)]
            for a in range(7):
                term = lines[a] * gs[0]
                for o in range(1, 4):
                    term = term + lines[o + a] * gs[o]
                slot = pl.multiple_of((h * 49 + a * 7 + b) * 8, 8)
                dacc[pl.ds(slot, 8), :] = dacc[pl.ds(slot, 8), :] + (term[:8] + term[8:])
        return 0

    def out_step(half, t, _):
        _, r, c, at = spot(t, rows, cols)
        total = conv_block(work, taps, half, at, True)
        for o in range(4):
            lanes = slice(half * 128, half * 128 + 128)
            res = total[o] + cot[r + o, pl.ds(c, 16), lanes].astype(F32)
            out[r + o, pl.ds(c, 16), lanes] = res.astype(BF16)
        return 0

    pieces = 6
    each = blocks // pieces
    for p in range(pieces):
        lax.fori_loop(p * each, (p + 1) * each, grad_step, 0)
        advance(due(len(events), p + 1, 2 * pieces - 1), 0, events)

    def fold(i, _):
        at = pl.multiple_of(i * 8, 8)
        dsend[0, pl.ds(i, 1), :] = jnp.sum(dacc[pl.ds(at, 8), :], axis=0, keepdims=True)
        return 0

    dsend[0, 96:104, :] = jnp.zeros((8, 128), F32)
    lax.fori_loop(0, halves * 49, fold, 0)
    d_events[0][0]()
    halo.finish(work)
    for p in range(pieces):
        lax.fori_loop(
            p * each, (p + 1) * each, functools.partial(out_step, p * halves // pieces), 0
        )
        advance(due(len(events), pieces + p + 1, 2 * pieces - 1), 0, events)
        advance(due(nb, p + 1, pieces - 1), 1, d_events)

    for k in range(wide):
        expand[:, k * 128 : (k + 1) * 128] = gathered[k * chans : (k + 1) * chans, :].astype(F32) * factor
        at = (wide + k) * chans
        part = gathered[at : at + chans, :].astype(F32) * factor
        reduce[k * 128 : (k + 1) * 128, :] = jnp.transpose(part)
    for h in range(halves):
        dw[:, h * 128 : (h + 1) * 128] = dsum[h * 49 : (h + 1) * 49, :] * factor


def both(one, two):
    one()
    two()


def strips(block):
    cols = block.shape[1]
    return (
        jnp.transpose(block[:, :3], (1, 0, 2)),
        jnp.transpose(block[:, cols - 3 :], (1, 0, 2)),
    )


def contract(left, right, ldim, rdim):
    return lax.dot_general(
        left, right, (((ldim,), (rdim,)), ((), ())), preferred_element_type=F32
    )


def mid_kernel(pre, cot, tissue, gain, shift, w_expand, b_expand, w_reduce, scale, grad, sums):
    rows, cols, chans = pre.shape
    hid = w_expand.shape[1]
    pixels = rows * cols
    turn = pl.program_id(0)

    @pl.when(turn == 0)
    def _():
        sums[...] = jnp.zeros_like(sums)

    masked = jnp.concatenate(
        [
            cot[:, k * TILE : (k + 1) * TILE, :].astype(F32) * tissue[turn, k].astype(F32)
            for k in range(cols // TILE)
        ],
        axis=1,
    ).reshape(pixels, chans)
    go_vals = (scale[...] * masked).astype(BF16)
    vals = pre[...].reshape(pixels, chans)
    center = vals - jnp.mean(vals, axis=-1, keepdims=True)
    rstd = lax.rsqrt(jnp.mean(center * center, axis=-1, keepdims=True) + 1e-06)
    nhat = center * rstd
    normed = (nhat * gain[...] + shift[...]).astype(BF16)
    go_t = jnp.transpose(go_vals)
    normed_t = jnp.transpose(normed)
    part = 256
    dnorm = None
    for k in range(hid // part):
        span = slice(k * part, (k + 1) * part)
        zvals = contract(normed, w_expand[:, span], 1, 0) + b_expand[:, span]
        cdf = 0.5 * (1.0 + lax.erf(zvals * 0.7071067811865476))
        hidden = (zvals * cdf).astype(BF16)
        slope = cdf + zvals * jnp.exp(-0.5 * zvals * zvals) * 0.3989422804014327
        dzvals = (contract(go_vals, w_reduce[span, :], 1, 1) * slope).astype(BF16)
        term = contract(dzvals, w_expand[:, span], 1, 1)
        dnorm = term if dnorm is None else dnorm + term
        to_expand = contract(normed_t, dzvals, 1, 0)
        to_reduce = contract(go_t, hidden, 1, 0)
        for j in range(part // 128):
            lanes = slice(j * 128, (j + 1) * 128)
            at = (k * (part // 128) + j) * chans
            sums[at : at + chans, :] += to_expand[:, lanes]
            at += hid // 128 * chans
            sums[at : at + chans, :] += to_reduce[:, lanes]
    dnorm = dnorm * gain[...]
    result = rstd * (
        dnorm
        - jnp.mean(dnorm, axis=-1, keepdims=True)
        - nhat * jnp.mean(dnorm * nhat, axis=-1, keepdims=True)
    )
    grad[...] = result.astype(BF16).reshape(rows, cols, chans)


def body(
    nty,
    ntx,
    block_input,
    cotangent,
    tissue,
    dw_weight,
    dw_bias,
    ln_gain,
    ln_bias,
    w_expand,
    b_expand,
    w_reduce,
    layer_scale,
):
    rows, cols, chans = block_input.shape
    hid = w_expand.shape[1]
    halves = chans // 128
    padded = halves * (rows + 6) * PITCH
    taps = jnp.transpose(dw_weight.reshape(49, halves, 128), (1, 0, 2)).reshape(halves * 49, 128)
    vmem = pl.BlockSpec(memory_space=pltpu.VMEM)
    flops = 49 * 2 * rows * cols * chans
    pre, xpad = pl.pallas_call(
        functools.partial(pre_kernel, nty, ntx),
        out_shape=(
            jax.ShapeDtypeStruct((rows, cols, chans), F32),
            jax.ShapeDtypeStruct((padded, 128), F32),
        ),
        in_specs=[vmem] * 5,
        out_specs=(vmem, vmem),
        scratch_shapes=halo_bufs(cols, rows, chans),
        compiler_params=pltpu.CompilerParams(
            collective_id=0, has_side_effects=True, vmem_limit_bytes=24 << 20
        ),
        cost_estimate=pl.CostEstimate(flops=flops, bytes_accessed=16 << 20, transcendentals=0),
        name="pre",
    )(block_input, *strips(block_input), taps, dw_bias.reshape(halves, 128))

    wide = hid // 128
    unit = nty * ntx * 32
    size = -(-2 * wide * chans // unit) * unit
    one = lambda array: pl.BlockSpec(array.shape, lambda i: (0,) * array.ndim)
    per_tile = pl.BlockSpec((TILE, cols, chans), lambda i: (i, 0, 0))
    whole = [
        ln_gain.reshape(1, chans),
        ln_bias.reshape(1, chans),
        w_expand,
        b_expand.reshape(1, hid),
        w_reduce,
        layer_scale.reshape(1, chans),
    ]
    grad_core, sums_in = pl.pallas_call(
        mid_kernel,
        grid=(rows // TILE,),
        out_shape=(
            jax.ShapeDtypeStruct((rows, cols, chans), BF16),
            jax.ShapeDtypeStruct((size, 128), F32),
        ),
        in_specs=[per_tile, per_tile, pl.BlockSpec(memory_space=pltpu.SMEM)]
        + [one(array) for array in whole],
        out_specs=(per_tile, pl.BlockSpec((size, 128), lambda i: (0, 0))),
        compiler_params=pltpu.CompilerParams(vmem_limit_bytes=36 << 20),
        cost_estimate=pl.CostEstimate(
            flops=10 * rows * cols * chans * hid,
            bytes_accessed=12 << 20,
            transcendentals=2 * rows * cols * hid,
        ),
        name="mid",
    )(pre, cotangent, tissue, *whole)

    factor = 1.0 / math.sqrt(rows * nty * cols * ntx)
    nb = (nty * ntx).bit_length() - 1
    return pl.pallas_call(
        functools.partial(post_kernel, nty, ntx, size, wide, factor),
        out_shape=(
            jax.ShapeDtypeStruct((rows, cols, chans), BF16),
            jax.ShapeDtypeStruct((49, chans), F32),
            jax.ShapeDtypeStruct((chans, hid), F32),
            jax.ShapeDtypeStruct((hid, chans), F32),
        ),
        in_specs=[vmem] * 7,
        out_specs=(vmem,) * 4,
        scratch_shapes=[
            pltpu.VMEM((size, 128), F32),
            pltpu.VMEM((104, 128), F32),
            pltpu.VMEM((padded, 128), F32),
            pltpu.VMEM((halves * 49 * 8, 128), F32),
            pltpu.VMEM((size, 128), BF16),
            pltpu.VMEM((size, 128), BF16),
            pltpu.VMEM((size, 128), BF16),
            pltpu.VMEM((nb, 104, 128), F32),
            pltpu.VMEM((nb, 104, 128), F32),
            pltpu.SemaphoreType.DMA((4 * nb,)),
            pltpu.SemaphoreType.DMA((4 * nb,)),
            pltpu.SemaphoreType.DMA((nb,)),
            pltpu.SemaphoreType.DMA((nb,)),
        ]
        + halo_bufs(cols, rows, chans),
        compiler_params=pltpu.CompilerParams(
            collective_id=1, has_side_effects=True, vmem_limit_bytes=36 << 20
        ),
        cost_estimate=pl.CostEstimate(flops=2 * flops, bytes_accessed=24 << 20, transcendentals=0),
        name="post",
    )(grad_core, *strips(grad_core), xpad, cotangent, taps, sums_in)


def solution(mesh):
    placed = (P("ty", "tx", None), P("ty", "tx", None), P("ty", "tx")) + (P(),) * 8
    return jax.shard_map(
        functools.partial(body, mesh.shape["ty"], mesh.shape["tx"]),
        mesh=mesh,
        in_specs=placed,
        out_specs=(P("ty", "tx", None), P(), P(), P()),
        check_vma=False,
    )
```
